32 devices in a mesh: groups: 2 (over y), context: 4 (over z), tensor: 4 (over x, core).
Axes of the slice: x: 2, y: 2, z: 4, core: 2. Of those that a mesh axis runs over, the one named last changes fastest.
Arguments:
- inputs: bfloat16 [4096, 1024], P(('groups', 'context')), parts along dimension 0, may hold values from -6 to 6
- frame_valid: int32 [4096], P(('groups', 'context')), parts along dimension 0, may hold values from 0 to 1, as said below
- norm1_gain: float32 [1024], replicated, may hold values from 0.1 to 1.9
- w_query: bfloat16 [1024, 1024], P(None, 'tensor')
- w_key: bfloat16 [1024, 1024], P(None, 'tensor')
- w_value: bfloat16 [1024, 1024], P(None, 'tensor'), may hold values from -0.1875 to 0.1875
- w_out: bfloat16 [1024, 1024], P('tensor'), may hold values from -0.1875 to 0.1875
- norm2_gain: float32 [1024], replicated, may hold values from 0.1 to 1.9
- w_point1: bfloat16 [2, 1024, 1024], P(None, None, 'tensor'), may hold values from -0.1875 to 0.1875
- w_depth: float32 [31, 1024], P(None, 'tensor'), may hold values from -1.5 to 1.5
- bn_scale: float32 [1024], P('tensor'), may hold values from 0.1 to 1.9
- bn_shift: float32 [1024], P('tensor'), may hold values from -1 to 1
- w_point2: bfloat16 [1024, 1024], P('tensor'), may hold values from -0.1875 to 0.1875
Outputs:
- output: bfloat16 [4096, 1024], P(('groups', 'context', 'tensor')), parts along dimension 0
The draws below stay inside these ranges and needn't reach their ends.
There are 2 independent parts, one for each index of `groups`. The reference program is written for one: setup_inputs(seed, part) draws one part's arguments, and reference() takes and returns one part's arrays. A program takes and returns all parts, laid end to end along the dimension named above; an argument that names none is the same for every part. Nothing has to cross between parts.
Inputs may be any that keep to these rules, and one draw needn't show every extreme that they name: `frame_valid`: the transcript frames form a prefix of the window of at least 1024 frames, followed by at least one padded frame.
All inputs are finite; a program needn't handle non-finite values.
Results may differ from the reference program's by a relative error of at most 0.0095.
Values may be sent and summed in bfloat16 or wider, within the bound.
A program may use at most 64 MiB of HBM per device.

```python
import math
import jax
import jax.numpy as jnp
from jax import lax

D = 1024
HEADS = 16
HD = 64
KERNEL = 31
F_DEV = 512
FRAMES = 2048
N_CONTEXT = 4


def draw_frame_valid(key, part):
    length = jax.random.randint(jax.random.fold_in(key, 3), (), FRAMES // 2, FRAMES)
    return (jnp.arange(FRAMES) < length).astype(jnp.int32)


def shared_base(key):
    return jax.random.normal(jax.random.fold_in(key, 7), (D, HEADS * HD), jnp.float32) / math.sqrt(D)


def draw_w_key(key, part):
    return shared_base(key).astype(jnp.bfloat16)


def draw_w_query(key, part):
    noise = jax.random.normal(jax.random.fold_in(key, 13), (D, HEADS * HD), jnp.float32) / math.sqrt(D)
    return (3.0 * noise).astype(jnp.bfloat16)


def level_of(rng, dims, pieces, least, largest):
    loudness, own = 1.0, jax.random.fold_in(rng, 6)
    for position, blocks in pieces:
        heights = jnp.exp(jax.random.uniform(jax.random.fold_in(own, position), (blocks,), jnp.float32, least / len(pieces), largest / len(pieces)))
        loudness = loudness * jnp.repeat(heights, dims[position] // blocks).reshape([-1 if axis == position else 1 for axis in range(len(dims))])
    return loudness


def centred(stream_key, shape, scale, limit, shards=(), dtype=jnp.bfloat16):
    entries = jax.random.normal(stream_key, shape, jnp.float32) * scale
    if len(shards) > 0:
        entries = level_of(stream_key, shape, shards, -0.22, 0.18) * entries
    return jnp.clip(entries, min=-limit, max=limit).astype(dtype)


def setup_inputs(seed: int = 0, part: int = 0) -> dict:
    seeds = jax.random.split(jax.random.key(seed), 14)
    own_keys = jax.random.split(jax.random.fold_in(seeds[13], part), 14)
    inputs = centred(own_keys[0], (FRAMES, D), 1.0, 6.0, ((0, 4),))
    frame_valid = draw_frame_valid(jax.random.fold_in(jax.random.fold_in(seeds[13], part), 71), part)
    norm1_gain = jnp.clip(1.0 + 0.18 * jax.random.normal(seeds[2], (D,), jnp.float32), 0.1, 1.9)
    w_query = draw_w_query(jax.random.fold_in(seeds[13], 71), part)
    w_key = draw_w_key(jax.random.fold_in(seeds[13], 71), part)
    w_value = centred(seeds[5], (D, HEADS * HD), D ** -0.5, 0.1875, ((1, 4),))
    w_out = centred(seeds[6], (HEADS * HD, D), (HEADS * HD) ** -0.5, 0.1875, ((0, 4),))
    norm2_gain = jnp.clip(1.0 + 0.18 * jax.random.normal(seeds[7], (D,), jnp.float32), 0.1, 1.9)
    w_point1 = centred(seeds[8], (2, D, D), D ** -0.5, 0.1875, ((2, 4),))
    w_depth = centred(seeds[9], (KERNEL, D), (KERNEL // 2) ** -0.5, 1.5, ((1, 4),), jnp.float32)
    bn_scale = jnp.clip(1.0 + 0.18 * jax.random.normal(seeds[10], (D,), jnp.float32), 0.1, 1.9)
    bn_shift = jnp.clip(jax.random.uniform(seeds[11], (D,), jnp.float32, -1.0, 1.0) * level_of(seeds[11], (D,), ((0, 4),), -0.4, 0.0), -1.0, 1.0)
    w_point2 = centred(seeds[12], (D, D), D ** -0.5, 0.1875, ((0, 4),))
    return {"inputs": inputs, "frame_valid": frame_valid, "norm1_gain": norm1_gain, "w_query": w_query, "w_key": w_key, "w_value": w_value, "w_out": w_out, "norm2_gain": norm2_gain, "w_point1": w_point1, "w_depth": w_depth, "bn_scale": bn_scale, "bn_shift": bn_shift, "w_point2": w_point2}


NEG = -1e+30

def normalize(rows, gain):
    values = rows.astype(jnp.float32)
    center = lax.optimization_barrier(jnp.mean(values, axis=-1, keepdims=True))
    spread = lax.optimization_barrier(jnp.mean(jnp.square(values - center), axis=-1, keepdims=True))
    return ((values - center) * lax.rsqrt(spread + 1e-05) * gain).astype(jnp.bfloat16)

def rounded(values):
    return lax.optimization_barrier(values.astype(jnp.bfloat16))

def reference(inputs, frame_valid, norm1_gain, w_query, w_key, w_value, w_out, norm2_gain, w_point1, w_depth, bn_scale, bn_shift, w_point2):
    normed = normalize(inputs, norm1_gain)
    query = rounded(jnp.dot(normed, w_query, preferred_element_type=jnp.float32))
    keys = rounded(jnp.dot(normed, w_key, preferred_element_type=jnp.float32))
    vals = rounded(jnp.dot(normed, w_value, preferred_element_type=jnp.float32))
    key_heads = keys.astype(jnp.float32).reshape(FRAMES, HEADS, HD)
    val_heads = vals.astype(jnp.float32).reshape(FRAMES, HEADS, HD)
    live = (frame_valid > 0)[None, None, :]
    query_blocks = query.astype(jnp.float32).reshape(N_CONTEXT, F_DEV, HEADS, HD)
    scale = 1.0 / HD ** 0.5

    def attend(block):
        scores = jnp.einsum('qhd,khd->hqk', block, key_heads) * scale
        scores = jnp.where(live, scores, NEG)
        top = lax.optimization_barrier(jnp.max(scores, axis=-1, keepdims=True))
        weights = jnp.where(live, jnp.exp(scores - top), 0.0)
        total = lax.optimization_barrier(jnp.sum(weights, axis=-1))
        light = rounded(weights).astype(jnp.float32)
        mixed = jnp.einsum('hqk,khd->qhd', light, val_heads)
        return (mixed / total.T[:, :, None]).reshape(F_DEV, HEADS * HD)
    attended = rounded(lax.map(attend, query_blocks).reshape(FRAMES, HEADS * HD))
    residual = rounded(inputs.astype(jnp.float32) + jnp.dot(attended, w_out, preferred_element_type=jnp.float32))
    normed_two = normalize(residual, norm2_gain)
    value_half = jnp.dot(normed_two, w_point1[0], preferred_element_type=jnp.float32)
    gate_half = jnp.dot(normed_two, w_point1[1], preferred_element_type=jnp.float32)
    gated = jnp.where((frame_valid > 0)[:, None], value_half * jax.nn.sigmoid(gate_half), 0.0)
    gated = rounded(gated).astype(jnp.float32)
    half = (KERNEL - 1) // 2
    padded = jnp.pad(gated, ((half, half), (0, 0)))
    depth = jnp.zeros((FRAMES, D), jnp.float32)
    for tap in range(KERNEL):
        depth = depth + padded[tap:tap + FRAMES] * w_depth[tap]
    activated = jax.nn.silu(depth * bn_scale + bn_shift).astype(jnp.bfloat16)
    mixed = jnp.dot(activated, w_point2, preferred_element_type=jnp.float32)
    return (residual.astype(jnp.float32) + mixed).astype(jnp.bfloat16)
```

```python
import functools
import math

import jax
import jax.numpy as jnp
from jax import lax
from jax.experimental import pallas as pl
from jax.experimental.pallas import tpu as pltpu
from jax.sharding import PartitionSpec as P

HD = 64
NEG = -1e30
PAIR = 128
MESH = pl.DeviceIdType.MESH


def normalize(rows, gain):
    values = rows.astype(jnp.float32)
    center = jnp.mean(values, axis=-1, keepdims=True)
    moved = values - center
    spread = jnp.mean(jnp.square(moved), axis=-1, keepdims=True)
    return (moved * lax.rsqrt(spread + 1e-05) * gain).astype(jnp.bfloat16)


def dot(a, b):
    return jnp.dot(a, b, preferred_element_type=jnp.float32)


class Line:
    def __init__(self, axis, count, slots, send_sems, recv_sems):
        self.axis, self.count, self.slots = axis, count, slots
        self.send_sems, self.recv_sems = send_sems, recv_sems
        self.me = lax.axis_index(axis)

    def sent(self, way, step):
        if way == 0:
            return self.me - step, (self.me >= step) & (self.me < self.count - 1)
        return self.me + step, (self.me + step < self.count) & (self.me > 0)

    def got(self, way, step):
        if way == 0:
            return self.me - 1 - step, self.me >= 1 + step
        return self.me + 1 + step, self.me + 1 + step < self.count

    def copy(self, way, step, slot):
        other = self.me + 1 if way == 0 else self.me + self.count - 1
        return pltpu.make_async_remote_copy(
            src_ref=self.slots.at[slot],
            dst_ref=self.slots.at[slot],
            send_sem=self.send_sems.at[way, step],
            recv_sem=self.recv_sems.at[way, step],
            device_id={self.axis: lax.rem(other, self.count)},
            device_id_type=MESH,
        )

    def start(self, way, step):
        slot, live = self.sent(way, step)

        @pl.when(live)
        def _():
            self.copy(way, step, slot).start()

    def wait_send(self, way, step):
        slot, live = self.sent(way, step)

        @pl.when(live)
        def _():
            self.copy(way, step, slot).wait_send()

    def wait_recv(self, way, step):
        slot, live = self.got(way, step)

        @pl.when(live)
        def _():
            self.copy(way, step, slot).wait_recv()

        return slot, live

    def finish(self):
        for way in range(2):

            @pl.loop(0, self.count - 1)
            def _(step):
                self.wait_send(way, step)


def kernel(
    n_ctx,
    n_ten,
    x_ref,
    mask_ref,
    valid_ref,
    gain1_ref,
    wq_ref,
    wk_ref,
    wv_ref,
    wo_ref,
    gain2_ref,
    wp1_ref,
    wd_ref,
    bns_ref,
    bnb_ref,
    wp2_ref,
    out_ref,
    normed,
    qm,
    kv,
    wo_all,
    wp2_all,
    att,
    acc,
    top,
    total,
    res,
    gpad,
    g32,
    act,
    act_all,
    kv_ss,
    kv_rs,
    wo_ss,
    wo_rs,
    wp_ss,
    wp_rs,
    at_ss,
    at_rs,
    halo_ss,
    halo_rs,
    act_ss,
    act_rs,
):
    ctx = lax.axis_index("context")
    ten = lax.axis_index("tensor")
    frames, width = x_ref.shape
    cols = wq_ref.shape[1]
    pairs = cols // PAIR
    share = frames // n_ten
    chunk = min(frames, 128)

    barrier = pltpu.get_barrier_semaphore()
    for shift in (1, n_ctx - 1):
        pl.semaphore_signal(
            barrier, inc=1, device_id={"context": lax.rem(ctx + shift, n_ctx)}, device_id_type=MESH
        )
    for shift in range(1, n_ten):
        pl.semaphore_signal(
            barrier, inc=1, device_id={"tensor": lax.rem(ten + shift, n_ten)}, device_id_type=MESH
        )
    kv_line = Line("context", n_ctx, kv, kv_ss, kv_rs)
    wo_line = Line("tensor", n_ten, wo_all, wo_ss, wo_rs)
    wp_line = Line("tensor", n_ten, wp2_all, wp_ss, wp_rs)
    at_line = Line("tensor", n_ten, att, at_ss, at_rs)

    wo_all[ten] = wo_ref[...]
    wp2_all[ten] = wp2_ref[...]

    @pl.loop(0, frames // chunk)
    def _(i):
        rows = pl.ds(pl.multiple_of(i * chunk, chunk), chunk)
        normed[rows, :] = normalize(x_ref[rows, :], gain1_ref[...])

    big = min(frames, 256)

    @pl.loop(0, frames // big)
    def _(i):
        rows = pl.ds(pl.multiple_of(i * big, big), big)
        low = pl.ds(pl.multiple_of(frames + i * big, big), big)
        kv[ctx, rows, :] = dot(normed[rows, :], wk_ref[...]).astype(jnp.bfloat16)
        kv[ctx, low, :] = dot(normed[rows, :], wv_ref[...]).astype(jnp.bfloat16)

    kv[ctx, 2 * frames :, :] = mask_ref[...]

    pl.semaphore_wait(barrier, 2 + n_ten - 1)
    for way in range(2):
        kv_line.start(way, 0)
    for way in range(2):
        wo_line.start(way, 0)
    for way in range(2):
        wp_line.start(way, 0)

    lane = lax.broadcasted_iota(jnp.int32, (1, PAIR), 1)
    halves = (lane < HD, lane >= HD)

    @pl.loop(0, frames // big)
    def _(i):
        rows = pl.ds(pl.multiple_of(i * big, big), big)
        query = (dot(normed[rows, :], wq_ref[...]).astype(jnp.bfloat16)) * jnp.bfloat16(
            1.0 / math.sqrt(HD)
        )
        for p in range(pairs):
            part = query[:, p * PAIR : (p + 1) * PAIR]
            for h in range(2):
                qm[2 * p + h, rows, :] = jnp.where(halves[h], part, jnp.bfloat16(0))

    top[...] = jnp.full_like(top, NEG)
    acc[...] = jnp.zeros_like(acc)

    def attend(block):
        strip = kv[block, 2 * frames :, :].astype(jnp.float32)
        bias = jnp.concatenate([strip[i : i + 1, :] for i in range(frames // cols)], axis=1)
        for p in range(pairs):
            span = slice(p * PAIR, (p + 1) * PAIR)
            keys = kv[block, :frames, span]
            vals = kv[block, frames : 2 * frames, span]
            for h in range(2):
                head = 2 * p + h
                mixed_vals = jnp.where(halves[h], vals, jnp.bfloat16(1))

                @pl.loop(0, frames // big)
                def _(i):
                    rows = pl.ds(pl.multiple_of(i * big, big), big)
                    scores = (
                        lax.dot_general(
                            qm[head, rows, :],
                            keys,
                            (((1,), (1,)), ((), ())),
                            preferred_element_type=jnp.float32,
                        )
                        + bias
                    )
                    old = top[head, rows, :1]
                    new = jnp.maximum(old, jnp.max(scores, axis=1, keepdims=True))
                    weights = jnp.exp(scores - new).astype(jnp.bfloat16)
                    acc[head, rows, :] = acc[head, rows, :] * jnp.exp(old - new) + dot(
                        weights, mixed_vals
                    )
                    top[head, rows, :] = jnp.broadcast_to(new, (big, PAIR))

    attend(ctx)

    def weight_step(step):
        for line in (wo_line, wp_line):
            for way in range(2):
                line.wait_recv(way, step)

                @pl.when(step + 1 < n_ten - 1)
                def _():
                    line.start(way, step + 1)

    @pl.loop(0, n_ctx - 1)
    def _(step):
        for way in range(2):
            kv_line.wait_recv(way, step)

            @pl.when(step + 1 < n_ctx - 1)
            def _():
                kv_line.start(way, step + 1)

        @pl.when(step < n_ten - 1)
        def _():
            weight_step(step)

        for way in range(2):
            slot, live = kv_line.got(way, step)

            @pl.when(live)
            def _():
                attend(slot)

    for step in range(n_ctx - 1, n_ten - 1):
        weight_step(step)

    @pl.loop(0, frames // big)
    def _(i):
        rows = pl.ds(pl.multiple_of(i * big, big), big)
        for p in range(pairs):
            first, second = acc[2 * p, rows, :], acc[2 * p + 1, rows, :]
            joined = jnp.where(
                halves[0], first / first[:, HD : HD + 1], second / second[:, :1]
            )
            att[ten, rows, p * PAIR : (p + 1) * PAIR] = joined.astype(jnp.bfloat16)

    for way in range(2):
        at_line.start(way, 0)

    def project(slot, first):
        @pl.loop(0, frames // big)
        def _(i):
            rows = pl.ds(pl.multiple_of(i * big, big), big)
            base = x_ref[rows, :].astype(jnp.float32) if first else total[rows, :]
            total[rows, :] = base + dot(att[slot, rows, :], wo_all[slot])

    project(ten, True)
    for step in range(n_ten - 1):
        for way in range(2):
            at_line.wait_recv(way, step)
            if step + 1 < n_ten - 1:
                at_line.start(way, step + 1)
        for way in range(2):
            slot, live = at_line.got(way, step)

            @pl.when(live)
            def _():
                project(slot, False)

    @pl.loop(0, frames // chunk)
    def _(i):
        rows = pl.ds(pl.multiple_of(i * chunk, chunk), chunk)
        rounded = total[rows, :].astype(jnp.bfloat16)
        res[rows, :] = rounded
        normed[rows, :] = normalize(rounded, gain2_ref[...])

    edge = (gpad.shape[0] - frames) // 2

    @pl.loop(0, frames // chunk)
    def _(i):
        rows = pl.ds(pl.multiple_of(i * chunk, chunk), chunk)
        spot = pl.ds(pl.multiple_of(edge + i * chunk, 16), chunk)
        value = dot(normed[rows, :], wp1_ref[0])
        gate = dot(normed[rows, :], wp1_ref[1])
        gated = jnp.where(valid_ref[rows, :] > 0, value * jax.nn.sigmoid(gate), 0.0)
        gpad[spot, :] = gated.astype(jnp.bfloat16)

    def halo(way):
        source = pl.ds(frames, edge) if way == 0 else pl.ds(edge, edge)
        target = pl.ds(0, edge) if way == 0 else pl.ds(frames + edge, edge)
        other = ctx + 1 if way == 0 else ctx + n_ctx - 1
        return pltpu.make_async_remote_copy(
            src_ref=gpad.at[source],
            dst_ref=gpad.at[target],
            send_sem=halo_ss.at[way],
            recv_sem=halo_rs.at[way],
            device_id={"context": lax.rem(other, n_ctx)},
            device_id_type=MESH,
        )

    sends = (ctx < n_ctx - 1, ctx > 0)
    gets = (ctx > 0, ctx < n_ctx - 1)
    for way in range(2):

        @pl.when(sends[way])
        def _():
            halo(way).start()

        @pl.when(jnp.logical_not(gets[way]))
        def _():
            at = 0 if way == 0 else frames + edge
            gpad[at : at + edge, :] = jnp.zeros((edge, cols), jnp.bfloat16)

    g32[edge : edge + frames, :] = gpad[edge : edge + frames, :].astype(jnp.float32)
    for way in range(2):

        @pl.when(gets[way])
        def _():
            halo(way).wait_recv()

        at = 0 if way == 0 else frames + edge
        g32[at : at + edge, :] = gpad[at : at + edge, :].astype(jnp.float32)

    taps = wd_ref.shape[0]
    half = (taps - 1) // 2
    some = min(frames, 64)

    @pl.loop(0, frames // some)
    def _(i):
        start = pl.multiple_of(i * some, some)
        window = g32[pl.ds(start, some + 2 * edge), :]
        depth = jnp.zeros((some, cols), jnp.float32)
        for tap in range(taps):
            at = edge - half + tap
            depth = depth + window[at : at + some, :] * wd_ref[tap : tap + 1, :]
        depth = depth * bns_ref[...] + bnb_ref[...]
        act[pl.ds(start, some), :] = jax.nn.silu(depth).astype(jnp.bfloat16)

    def part(peer):
        return pl.ds(pl.multiple_of(peer * share, share), share)

    def swap(shift):
        peer = lax.rem(ten + shift, n_ten)
        return pltpu.make_async_remote_copy(
            src_ref=act.at[part(peer)],
            dst_ref=act_all.at[shift],
            send_sem=act_ss.at[shift],
            recv_sem=act_rs.at[shift],
            device_id={"tensor": peer},
            device_id_type=MESH,
        )

    for shift in range(1, n_ten):
        swap(shift).start()
    mine = part(ten)
    out = res[mine, :].astype(jnp.float32)
    out = out + dot(act[mine, :], wp2_all[ten])
    for shift in range(1, n_ten):
        swap(shift).wait_recv()
        out = out + dot(act_all[shift], wp2_all[lax.rem(ten + n_ten - shift, n_ten)])
    out_ref[...] = out.astype(jnp.bfloat16)

    for line in (kv_line, wo_line, wp_line, at_line):
        line.finish()
    for way in range(2):

        @pl.when(sends[way])
        def _():
            halo(way).wait_send()

    for shift in range(1, n_ten):
        swap(shift).wait_send()


def local(
    n_ctx,
    n_ten,
    inputs,
    frame_valid,
    norm1_gain,
    w_query,
    w_key,
    w_value,
    w_out,
    norm2_gain,
    w_point1,
    w_depth,
    bn_scale,
    bn_shift,
    w_point2,
):
    frames, width = inputs.shape
    cols = w_query.shape[1]
    heads = cols // HD
    share = frames // n_ten
    strips = frames // cols
    edge = 16
    mask = jnp.where(frame_valid > 0, 0.0, NEG).astype(jnp.bfloat16).reshape(strips, cols)
    mask = jnp.pad(mask, ((0, 16 - strips), (0, 0)))
    valid = frame_valid.astype(jnp.float32)[:, None]
    bf, f32 = jnp.bfloat16, jnp.float32
    sem = pltpu.SemaphoreType.DMA
    line = [sem((2, n_ctx - 1))] * 2 + [sem((2, n_ten - 1))] * 6
    return pl.pallas_call(
        functools.partial(kernel, n_ctx, n_ten),
        out_shape=jax.ShapeDtypeStruct((share, width), bf),
        in_specs=[pl.BlockSpec(memory_space=pltpu.VMEM)] * 14,
        out_specs=pl.BlockSpec(memory_space=pltpu.VMEM),
        scratch_shapes=[
            pltpu.VMEM((frames, width), bf),
            pltpu.VMEM((heads, frames, PAIR), bf),
            pltpu.VMEM((n_ctx, 2 * frames + 16, cols), bf),
            pltpu.VMEM((n_ten, cols, width), bf),
            pltpu.VMEM((n_ten, cols, width), bf),
            pltpu.VMEM((n_ten, frames, cols), bf),
            pltpu.VMEM((heads, frames, PAIR), f32),
            pltpu.VMEM((heads, frames, PAIR), f32),
            pltpu.VMEM((frames, width), f32),
            pltpu.VMEM((frames, width), bf),
            pltpu.VMEM((frames + 2 * edge, cols), bf),
            pltpu.VMEM((frames + 2 * edge, cols), f32),
            pltpu.VMEM((frames, cols), bf),
            pltpu.VMEM((n_ten, share, cols), bf),
        ]
        + line
        + [sem((2,)), sem((2,)), sem((n_ten,)), sem((n_ten,))],
        compiler_params=pltpu.CompilerParams(
            collective_id=0, has_side_effects=True, vmem_limit_bytes=50 * 1024 * 1024
        ),
    )(
        inputs,
        mask,
        valid,
        norm1_gain[None],
        w_query,
        w_key,
        w_value,
        w_out,
        norm2_gain[None],
        w_point1,
        w_depth,
        bn_scale[None],
        bn_shift[None],
        w_point2,
    )


def solution(mesh):
    placed = (
        P(("groups", "context"), None),
        P(("groups", "context")),
        P(),
        P(None, "tensor"),
        P(None, "tensor"),
        P(None, "tensor"),
        P("tensor", None),
        P(),
        P(None, None, "tensor"),
        P(None, "tensor"),
        P("tensor"),
        P("tensor"),
        P("tensor", None),
    )
    return jax.shard_map(
        functools.partial(local, mesh.shape["context"], mesh.shape["tensor"]),
        mesh=mesh,
        in_specs=placed,
        out_specs=P(("groups", "context", "tensor"), None),
        check_vma=False,
    )
```

```python
import functools
import math

import jax
import jax.numpy as jnp
from jax import lax
from jax.experimental import pallas as pl
from jax.experimental.pallas import tpu as pltpu
from jax.sharding import PartitionSpec as P

HD = 64
NEG = -1e30
PAIR = 128
MESH = pl.DeviceIdType.MESH


def normalize(rows, gain):
    values = rows.astype(jnp.float32)
    center = jnp.mean(values, axis=-1, keepdims=True)
    moved = values - center
    spread = jnp.mean(jnp.square(moved), axis=-1, keepdims=True)
    return (moved * lax.rsqrt(spread + 1e-05) * gain).astype(jnp.bfloat16)


def dot(a, b):
    return jnp.dot(a, b, preferred_element_type=jnp.float32)


class Line:
    def __init__(self, axis, count, pick, send_sems, recv_sems):
        self.axis, self.count, self.pick = axis, count, pick
        self.send_sems, self.recv_sems = send_sems, recv_sems
        self.me = lax.axis_index(axis)

    def sent(self, way, step):
        if way == 0:
            return self.me - step, (self.me >= step) & (self.me < self.count - 1)
        return self.me + step, (self.me + step < self.count) & (self.me > 0)

    def got(self, way, step):
        if way == 0:
            return self.me - 1 - step, self.me >= 1 + step
        return self.me + 1 + step, self.me + 1 + step < self.count

    def copy(self, way, step, slot):
        other = self.me + 1 if way == 0 else self.me + self.count - 1
        return pltpu.make_async_remote_copy(
            src_ref=self.pick(slot),
            dst_ref=self.pick(slot),
            send_sem=self.send_sems.at[way, step],
            recv_sem=self.recv_sems.at[way, step],
            device_id={self.axis: lax.rem(other, self.count)},
            device_id_type=MESH,
        )

    def start(self, way, step):
        slot, live = self.sent(way, step)

        @pl.when(live)
        def _():
            self.copy(way, step, slot).start()

    def wait_send(self, way, step):
        slot, live = self.sent(way, step)

        @pl.when(live)
        def _():
            self.copy(way, step, slot).wait_send()

    def wait_recv(self, way, step):
        slot, live = self.got(way, step)

        @pl.when(live)
        def _():
            self.copy(way, step, slot).wait_recv()

        return slot, live

    def finish(self):
        for way in range(2):

            @pl.loop(0, self.count - 1)
            def _(step):
                self.wait_send(way, step)


def kernel(
    n_ctx,
    n_ten,
    x_hbm,
    mask_ref,
    valid_ref,
    gain1_ref,
    wq_hbm,
    wk_hbm,
    wv_hbm,
    wo_hbm,
    gain2_ref,
    wp1_hbm,
    wd_ref,
    bns_ref,
    bnb_ref,
    wp2_hbm,
    out_ref,
    x_ref,
    wq_ref,
    wk_ref,
    wv_ref,
    wp1_ref,
    load,
    blocks,
    masks,
    normed,
    qm,
    kv,
    wo_all,
    wp2_all,
    att,
    acc,
    top,
    total,
    res,
    gpad,
    g32,
    act,
    act_all,
    kv_ss,
    kv_rs,
    mk_ss,
    mk_rs,
    bl_ss,
    bl_rs,
    wo_ss,
    wo_rs,
    wp_ss,
    wp_rs,
    at_ss,
    at_rs,
    halo_ss,
    halo_rs,
    act_ss,
    act_rs,
):
    ctx = lax.axis_index("context")
    ten = lax.axis_index("tensor")
    frames, width = x_ref.shape
    cols = wq_ref.shape[1]
    pairs = cols // PAIR
    share = frames // n_ten
    chunk = min(frames, 128)

    barrier = pltpu.get_barrier_semaphore()
    for shift in (1, n_ctx - 1):
        pl.semaphore_signal(
            barrier, inc=1, device_id={"context": lax.rem(ctx + shift, n_ctx)}, device_id_type=MESH
        )
    for shift in range(1, n_ten):
        pl.semaphore_signal(
            barrier, inc=1, device_id={"tensor": lax.rem(ten + shift, n_ten)}, device_id_type=MESH
        )
    loads = [
        pltpu.make_async_copy(source, target, load.at[i])
        for i, (source, target) in enumerate(
            (
                (x_hbm, x_ref),
                (wk_hbm, wk_ref),
                (wv_hbm, wv_ref),
                (wq_hbm, wq_ref),
                (wo_hbm, wo_all.at[ten]),
                (wp1_hbm, wp1_ref),
                (wp2_hbm, wp2_all.at[ten]),
            )
        )
    ]
    for item in loads:
        item.start()
    z_line = Line("context", n_ctx, lambda slot: blocks.at[slot, ten], kv_ss, kv_rs)
    mk_line = Line("context", n_ctx, lambda slot: masks.at[slot], mk_ss, mk_rs)
    wo_line = Line("tensor", n_ten, lambda slot: wo_all.at[slot], wo_ss, wo_rs)
    wp_line = Line("tensor", n_ten, lambda slot: wp2_all.at[slot], wp_ss, wp_rs)
    at_line = Line("tensor", n_ten, lambda slot: att.at[slot], at_ss, at_rs)

    def spread(block):
        return Line(
            "tensor",
            n_ten,
            lambda slot: blocks.at[block, slot],
            bl_ss.at[block],
            bl_rs.at[block],
        )

    masks[ctx] = mask_ref[...]
    loads[0].wait()

    def norm_part(i):
        rows = pl.ds(pl.multiple_of(i * share, share), share)
        blocks[ctx, i] = normalize(x_ref[rows, :], gain1_ref[...])

    norm_part(ten)
    pl.semaphore_wait(barrier, 2 + n_ten - 1)
    for line in (mk_line, z_line):
        for way in range(2):
            line.start(way, 0)
    loads[4].wait()
    for way in range(2):
        wo_line.start(way, 0)

    @pl.loop(1, n_ten)
    def _(shift):
        norm_part(lax.rem(ten + shift, n_ten))

    def project_kv(block, spot):
        @pl.loop(0, n_ten)
        def _(i):
            rows = pl.ds(pl.multiple_of(i * share, share), share)
            low = pl.ds(pl.multiple_of(frames + i * share, share), share)
            part = blocks[block, i]
            kv[spot, rows, :] = dot(part, wk_ref[...]).astype(jnp.bfloat16)
            kv[spot, low, :] = dot(part, wv_ref[...]).astype(jnp.bfloat16)

    big = min(frames, 256)
    lane = lax.broadcasted_iota(jnp.int32, (1, PAIR), 1)
    halves = (lane < HD, lane >= HD)

    for item in loads[1:4]:
        item.wait()
    project_kv(ctx, 0)

    @pl.loop(0, n_ten)
    def _(i):
        rows = pl.ds(pl.multiple_of(i * share, share), share)
        query = (dot(blocks[ctx, i], wq_ref[...]).astype(jnp.bfloat16)) * jnp.bfloat16(
            1.0 / math.sqrt(HD)
        )
        for p in range(pairs):
            part = query[:, p * PAIR : (p + 1) * PAIR]
            for h in range(2):
                qm[2 * p + h, rows, :] = jnp.where(halves[h], part, jnp.bfloat16(0))

    top[...] = jnp.full_like(top, NEG)
    acc[...] = jnp.zeros_like(acc)

    def attend(block, spot, p):
        strip = masks[block].astype(jnp.float32)
        bias = jnp.concatenate([strip[i : i + 1, :] for i in range(frames // cols)], axis=1)
        if True:
            span = slice(p * PAIR, (p + 1) * PAIR)
            keys = kv[spot, :frames, span]
            vals = kv[spot, frames : 2 * frames, span]
            for h in range(2):
                head = 2 * p + h
                mixed_vals = jnp.where(halves[h], vals, jnp.bfloat16(1))

                @pl.loop(0, frames // big)
                def _(i):
                    rows = pl.ds(pl.multiple_of(i * big, big), big)
                    scores = (
                        lax.dot_general(
                            qm[head, rows, :],
                            keys,
                            (((1,), (1,)), ((), ())),
                            preferred_element_type=jnp.float32,
                        )
                        + bias
                    )
                    old = top[head, rows, :1]
                    new = jnp.maximum(old, jnp.max(scores, axis=1, keepdims=True))
                    weights = jnp.exp(scores - new).astype(jnp.bfloat16)
                    acc[head, rows, :] = acc[head, rows, :] * jnp.exp(old - new) + dot(
                        weights, mixed_vals
                    )
                    top[head, rows, :] = jnp.broadcast_to(new, (big, PAIR))

    def weight_step(line, step):
        for way in range(2):
            line.wait_recv(way, step)

            @pl.when(step + 1 < n_ten - 1)
            def _():
                line.start(way, step + 1)

    def arrive(step):
        for way in range(2):
            mk_line.wait_recv(way, step)
            slot, live = z_line.wait_recv(way, step)

            @pl.when(step + 1 < n_ctx - 1)
            def _():
                z_line.start(way, step + 1)
                mk_line.start(way, step + 1)

            @pl.when(live)
            def _():
                for side in range(2):
                    spread(slot).start(side, 0)

    def relay(step, hop):
        for way in range(2):
            slot, live = z_line.got(way, step)

            @pl.when(live)
            def _():
                for side in range(2):
                    spread(slot).wait_recv(side, hop)
                    if hop + 1 < n_ten - 1:
                        spread(slot).start(side, hop + 1)

    def work(jobs, step):
        for p in range(pairs):
            for block, spot, live in jobs:
                pl.when(live)(lambda: attend(block, spot, p))
            hops = [p] if p < pairs - 1 else range(pairs - 1, n_ten - 2)
            for hop in hops:
                if hop < n_ten - 2:

                    @pl.when(step < n_ctx - 1)
                    def _():
                        relay(step, hop)

    arrive(0)
    work([(ctx, 0, ctx >= 0)], 0)

    @pl.loop(0, n_ctx - 1)
    def _(step):
        @pl.when(step + 1 < n_ctx - 1)
        def _():
            arrive(step + 1)

        @pl.when(step < n_ten - 1)
        def _():
            weight_step(wo_line, step)

        relay(step, n_ten - 2)
        jobs = []
        for way in range(2):
            slot, live = z_line.got(way, step)
            pl.when(live)(lambda: project_kv(slot, way))
            jobs.append((slot, way, live))
        work(jobs, step + 1)

    for step in range(n_ctx - 1, n_ten - 1):
        weight_step(wo_line, step)
    loads[5].wait()
    loads[6].wait()

    @pl.loop(0, frames // big)
    def _(i):
        rows = pl.ds(pl.multiple_of(i * big, big), big)
        for p in range(pairs):
            first, second = acc[2 * p, rows, :], acc[2 * p + 1, rows, :]
            joined = jnp.where(
                halves[0], first / first[:, HD : HD + 1], second / second[:, :1]
            )
            att[ten, rows, p * PAIR : (p + 1) * PAIR] = joined.astype(jnp.bfloat16)

    for way in range(2):
        at_line.start(way, 0)

    def project(slot, first):
        @pl.loop(0, frames // big)
        def _(i):
            rows = pl.ds(pl.multiple_of(i * big, big), big)
            base = x_ref[rows, :].astype(jnp.float32) if first else total[rows, :]
            total[rows, :] = base + dot(att[slot, rows, :], wo_all[slot])

    for way in range(2):
        wp_line.start(way, 0)
    project(ten, True)
    for step in range(n_ten - 1):
        for way in range(2):
            at_line.wait_recv(way, step)
            if step + 1 < n_ten - 1:
                at_line.start(way, step + 1)
        for way in range(2):
            slot, live = at_line.got(way, step)

            @pl.when(live)
            def _():
                project(slot, False)

    @pl.loop(0, frames // chunk)
    def _(i):
        rows = pl.ds(pl.multiple_of(i * chunk, chunk), chunk)
        rounded = total[rows, :].astype(jnp.bfloat16)
        res[rows, :] = rounded
        normed[rows, :] = normalize(rounded, gain2_ref[...])

    weight_step(wp_line, 0)
    edge = (gpad.shape[0] - frames) // 2

    @pl.loop(0, frames // chunk)
    def _(i):
        rows = pl.ds(pl.multiple_of(i * chunk, chunk), chunk)
        spot = pl.ds(pl.multiple_of(edge + i * chunk, 16), chunk)
        value = dot(normed[rows, :], wp1_ref[0])
        gate = dot(normed[rows, :], wp1_ref[1])
        gated = jnp.where(valid_ref[rows, :] > 0, value * jax.nn.sigmoid(gate), 0.0)
        gpad[spot, :] = gated.astype(jnp.bfloat16)

    def halo(way):
        source = pl.ds(frames, edge) if way == 0 else pl.ds(edge, edge)
        target = pl.ds(0, edge) if way == 0 else pl.ds(frames + edge, edge)
        other = ctx + 1 if way == 0 else ctx + n_ctx - 1
        return pltpu.make_async_remote_copy(
            src_ref=gpad.at[source],
            dst_ref=gpad.at[target],
            send_sem=halo_ss.at[way],
            recv_sem=halo_rs.at[way],
            device_id={"context": lax.rem(other, n_ctx)},
            device_id_type=MESH,
        )

    sends = (ctx < n_ctx - 1, ctx > 0)
    gets = (ctx > 0, ctx < n_ctx - 1)
    for way in range(2):

        @pl.when(sends[way])
        def _():
            halo(way).start()

        @pl.when(jnp.logical_not(gets[way]))
        def _():
            at = 0 if way == 0 else frames + edge
            gpad[at : at + edge, :] = jnp.zeros((edge, cols), jnp.bfloat16)

    if n_ten > 2:
        weight_step(wp_line, 1)
    g32[edge : edge + frames, :] = gpad[edge : edge + frames, :].astype(jnp.float32)
    for way in range(2):

        @pl.when(gets[way])
        def _():
            halo(way).wait_recv()

        at = 0 if way == 0 else frames + edge
        g32[at : at + edge, :] = gpad[at : at + edge, :].astype(jnp.float32)

    taps = wd_ref.shape[0]
    half = (taps - 1) // 2
    some = min(frames, 64)

    @pl.loop(0, frames // some)
    def _(i):
        start = pl.multiple_of(i * some, some)
        window = g32[pl.ds(start, some + 2 * edge), :]
        depth = jnp.zeros((some, cols), jnp.float32)
        for tap in range(taps):
            at = edge - half + tap
            depth = depth + window[at : at + some, :] * wd_ref[tap : tap + 1, :]
        depth = depth * bns_ref[...] + bnb_ref[...]
        act[pl.ds(start, some), :] = jax.nn.silu(depth).astype(jnp.bfloat16)

    def part(peer):
        return pl.ds(pl.multiple_of(peer * share, share), share)

    def swap(shift):
        peer = lax.rem(ten + shift, n_ten)
        return pltpu.make_async_remote_copy(
            src_ref=act.at[part(peer)],
            dst_ref=act_all.at[shift],
            send_sem=act_ss.at[shift],
            recv_sem=act_rs.at[shift],
            device_id={"tensor": peer},
            device_id_type=MESH,
        )

    for shift in range(1, n_ten):
        swap(shift).start()
    for step in range(2, n_ten - 1):
        weight_step(wp_line, step)
    mine = part(ten)
    out = res[mine, :].astype(jnp.float32)
    out = out + dot(act[mine, :], wp2_all[ten])
    for shift in range(1, n_ten):
        swap(shift).wait_recv()
        out = out + dot(act_all[shift], wp2_all[lax.rem(ten + n_ten - shift, n_ten)])
    out_ref[...] = out.astype(jnp.bfloat16)

    for line in (z_line, mk_line, wo_line, wp_line, at_line):
        line.finish()

    @pl.loop(0, n_ctx)
    def _(block):
        @pl.when(block != ctx)
        def _():
            spread(block).finish()

    for way in range(2):

        @pl.when(sends[way])
        def _():
            halo(way).wait_send()

    for shift in range(1, n_ten):
        swap(shift).wait_send()


def local(
    n_ctx,
    n_ten,
    inputs,
    frame_valid,
    norm1_gain,
    w_query,
    w_key,
    w_value,
    w_out,
    norm2_gain,
    w_point1,
    w_depth,
    bn_scale,
    bn_shift,
    w_point2,
):
    frames, width = inputs.shape
    cols = w_query.shape[1]
    heads = cols // HD
    share = frames // n_ten
    strips = frames // cols
    edge = 16
    mask = jnp.where(frame_valid > 0, 0.0, NEG).astype(jnp.bfloat16).reshape(strips, cols)
    mask = jnp.pad(mask, ((0, 16 - strips), (0, 0)))
    valid = frame_valid.astype(jnp.float32)[:, None]
    bf, f32 = jnp.bfloat16, jnp.float32
    sem = pltpu.SemaphoreType.DMA
    line = [sem((2, n_ctx - 1))] * 4 + [sem((n_ctx, 2, n_ten - 1))] * 2 + [sem((2, n_ten - 1))] * 6
    return pl.pallas_call(
        functools.partial(kernel, n_ctx, n_ten),
        out_shape=jax.ShapeDtypeStruct((share, width), bf),
        in_specs=[pl.BlockSpec(memory_space=pl.ANY if i in (0, 4, 5, 6, 7, 9, 13) else pltpu.VMEM) for i in range(14)],
        out_specs=pl.BlockSpec(memory_space=pltpu.VMEM),
        scratch_shapes=[
            pltpu.VMEM((frames, width), bf),
            pltpu.VMEM((width, cols), bf),
            pltpu.VMEM((width, cols), bf),
            pltpu.VMEM((width, cols), bf),
            pltpu.VMEM((2, width, cols), bf),
            sem((7,)),
            pltpu.VMEM((n_ctx, n_ten, share, width), bf),
            pltpu.VMEM((n_ctx, 16, cols), bf),
            pltpu.VMEM((frames, width), bf),
            pltpu.VMEM((heads, frames, PAIR), bf),
            pltpu.VMEM((2, 2 * frames, cols), bf),
            pltpu.VMEM((n_ten, cols, width), bf),
            pltpu.VMEM((n_ten, cols, width), bf),
            pltpu.VMEM((n_ten, frames, cols), bf),
            pltpu.VMEM((heads, frames, PAIR), f32),
            pltpu.VMEM((heads, frames, PAIR), f32),
            pltpu.VMEM((frames, width), f32),
            pltpu.VMEM((frames, width), bf),
            pltpu.VMEM((frames + 2 * edge, cols), bf),
            pltpu.VMEM((frames + 2 * edge, cols), f32),
            pltpu.VMEM((frames, cols), bf),
            pltpu.VMEM((n_ten, share, cols), bf),
        ]
        + line
        + [sem((2,)), sem((2,)), sem((n_ten,)), sem((n_ten,))],
        compiler_params=pltpu.CompilerParams(
            collective_id=0, has_side_effects=True, vmem_limit_bytes=60 * 1024 * 1024
        ),
    )(
        inputs,
        mask,
        valid,
        norm1_gain[None],
        w_query,
        w_key,
        w_value,
        w_out,
        norm2_gain[None],
        w_point1,
        w_depth,
        bn_scale[None],
        bn_shift[None],
        w_point2,
    )


def solution(mesh):
    placed = (
        P(("groups", "context"), None),
        P(("groups", "context")),
        P(),
        P(None, "tensor"),
        P(None, "tensor"),
        P(None, "tensor"),
        P("tensor", None),
        P(),
        P(None, None, "tensor"),
        P(None, "tensor"),
        P("tensor"),
        P("tensor"),
        P("tensor", None),
    )
    return jax.shard_map(
        functools.partial(local, mesh.shape["context"], mesh.shape["tensor"]),
        mesh=mesh,
        in_specs=placed,
        out_specs=P(("groups", "context", "tensor"), None),
        check_vma=False,
    )
```

```python
import functools
import math

import jax
import jax.numpy as jnp
from jax import lax
from jax.experimental import pallas as pl
from jax.experimental.pallas import tpu as pltpu
from jax.sharding import PartitionSpec as P

HD = 64
NEG = -1e30
PAIR = 128
MESH = pl.DeviceIdType.MESH


def normalize(rows, gain):
    values = rows.astype(jnp.float32)
    center = jnp.mean(values, axis=-1, keepdims=True)
    moved = values - center
    spread = jnp.mean(jnp.square(moved), axis=-1, keepdims=True)
    return (moved * lax.rsqrt(spread + 1e-05) * gain).astype(jnp.bfloat16)


def dot(a, b):
    return jnp.dot(a, b, preferred_element_type=jnp.float32)


class Line:
    def __init__(self, axis, count, pick, send_sems, recv_sems):
        self.axis, self.count, self.pick = axis, count, pick
        self.send_sems, self.recv_sems = send_sems, recv_sems
        self.me = lax.axis_index(axis)

    def sent(self, way, step):
        if way == 0:
            return self.me - step, (self.me >= step) & (self.me < self.count - 1)
        return self.me + step, (self.me + step < self.count) & (self.me > 0)

    def got(self, way, step):
        if way == 0:
            return self.me - 1 - step, self.me >= 1 + step
        return self.me + 1 + step, self.me + 1 + step < self.count

    def copy(self, way, step, slot):
        other = self.me + 1 if way == 0 else self.me + self.count - 1
        return pltpu.make_async_remote_copy(
            src_ref=self.pick(slot),
            dst_ref=self.pick(slot),
            send_sem=self.send_sems.at[way, step],
            recv_sem=self.recv_sems.at[way, step],
            device_id={self.axis: lax.rem(other, self.count)},
            device_id_type=MESH,
        )

    def start(self, way, step):
        slot, live = self.sent(way, step)

        @pl.when(live)
        def _():
            self.copy(way, step, slot).start()

    def wait_send(self, way, step):
        slot, live = self.sent(way, step)

        @pl.when(live)
        def _():
            self.copy(way, step, slot).wait_send()

    def wait_recv(self, way, step):
        slot, live = self.got(way, step)

        @pl.when(live)
        def _():
            self.copy(way, step, slot).wait_recv()

        return slot, live

    def finish(self):
        for way in range(2):

            @pl.loop(0, self.count - 1)
            def _(step):
                self.wait_send(way, step)


def kernel(
    n_ctx,
    n_ten,
    x_hbm,
    mask_ref,
    valid_ref,
    gain1_ref,
    wq_hbm,
    wk_hbm,
    wv_hbm,
    wo_hbm,
    gain2_ref,
    wp1_hbm,
    wd_ref,
    bns_ref,
    bnb_ref,
    wp2_hbm,
    out_ref,
    x_ref,
    wq_ref,
    wk_ref,
    wv_ref,
    wp1_ref,
    load,
    masks,
    normed,
    qm,
    kv,
    wo_all,
    wp2_all,
    att,
    acc,
    top,
    total,
    res,
    gpad,
    g32,
    act,
    act_all,
    kv_ss,
    kv_rs,
    mk_ss,
    mk_rs,
    wo_ss,
    wo_rs,
    wp_ss,
    wp_rs,
    at_ss,
    at_rs,
    halo_ss,
    halo_rs,
    act_ss,
    act_rs,
):
    ctx = lax.axis_index("context")
    ten = lax.axis_index("tensor")
    frames, width = x_ref.shape
    cols = wq_ref.shape[1]
    pairs = cols // PAIR
    share = frames // n_ten
    chunk = min(frames, 128)

    barrier = pltpu.get_barrier_semaphore()
    for shift in (1, n_ctx - 1):
        pl.semaphore_signal(
            barrier, inc=1, device_id={"context": lax.rem(ctx + shift, n_ctx)}, device_id_type=MESH
        )
    for shift in range(1, n_ten):
        pl.semaphore_signal(
            barrier, inc=1, device_id={"tensor": lax.rem(ten + shift, n_ten)}, device_id_type=MESH
        )
    loads = [
        pltpu.make_async_copy(source, target, load.at[i])
        for i, (source, target) in enumerate(
            (
                (x_hbm, x_ref),
                (wk_hbm, wk_ref),
                (wv_hbm, wv_ref),
                (wq_hbm, wq_ref),
                (wo_hbm, wo_all.at[ten]),
                (wp1_hbm, wp1_ref),
                (wp2_hbm, wp2_all.at[ten]),
            )
        )
    ]
    for item in loads:
        item.start()

    def pair_line(axis, count, slots, p, send_sems, recv_sems):
        return Line(axis, count, lambda slot: slots.at[slot, p], send_sems.at[p], recv_sems.at[p])

    kv_lines = [pair_line("context", n_ctx, kv, p, kv_ss, kv_rs) for p in range(pairs)]
    at_lines = [pair_line("tensor", n_ten, att, p, at_ss, at_rs) for p in range(pairs)]
    mk_line = Line("context", n_ctx, lambda slot: masks.at[slot], mk_ss, mk_rs)
    wo_line = Line("tensor", n_ten, lambda slot: wo_all.at[slot], wo_ss, wo_rs)
    wp_line = Line("tensor", n_ten, lambda slot: wp2_all.at[slot], wp_ss, wp_rs)
    masks[ctx] = mask_ref[...]
    loads[0].wait()

    @pl.loop(0, frames // chunk)
    def _(i):
        rows = pl.ds(pl.multiple_of(i * chunk, chunk), chunk)
        normed[rows, :] = normalize(x_ref[rows, :], gain1_ref[...])

    big = min(frames, 256)
    loads[1].wait()
    loads[2].wait()

    @pl.loop(0, frames // big)
    def _(i):
        rows = pl.ds(pl.multiple_of(i * big, big), big)
        low = pl.ds(pl.multiple_of(frames + i * big, big), big)
        keys = dot(normed[rows, :], wk_ref[...]).astype(jnp.bfloat16)
        vals = dot(normed[rows, :], wv_ref[...]).astype(jnp.bfloat16)
        for p in range(pairs):
            kv[ctx, p, rows, :] = keys[:, p * PAIR : (p + 1) * PAIR]
            kv[ctx, p, low, :] = vals[:, p * PAIR : (p + 1) * PAIR]

    pl.semaphore_wait(barrier, 2 + n_ten - 1)
    for line in [mk_line] + kv_lines:
        for way in range(2):
            line.start(way, 0)
    loads[4].wait()
    loads[6].wait()
    for line in (wo_line, wp_line):
        for way in range(2):
            line.start(way, 0)
    loads[3].wait()

    lane = lax.broadcasted_iota(jnp.int32, (1, PAIR), 1)
    halves = (lane < HD, lane >= HD)

    @pl.loop(0, frames // big)
    def _(i):
        rows = pl.ds(pl.multiple_of(i * big, big), big)
        query = (dot(normed[rows, :], wq_ref[...]).astype(jnp.bfloat16)) * jnp.bfloat16(
            1.0 / math.sqrt(HD)
        )
        for p in range(pairs):
            part = query[:, p * PAIR : (p + 1) * PAIR]
            for h in range(2):
                qm[2 * p + h, rows, :] = jnp.where(halves[h], part, jnp.bfloat16(0))

    top[...] = jnp.full_like(top, NEG)
    acc[...] = jnp.zeros_like(acc)

    def attend(block, p):
        strip = masks[block].astype(jnp.float32)
        bias = jnp.concatenate([strip[i : i + 1, :] for i in range(frames // cols)], axis=1)
        if True:
            keys = kv[block, p, :frames, :]
            vals = kv[block, p, frames:, :]
            for h in range(2):
                head = 2 * p + h
                mixed_vals = jnp.where(halves[h], vals, jnp.bfloat16(1))

                @pl.loop(0, frames // big)
                def _(i):
                    rows = pl.ds(pl.multiple_of(i * big, big), big)
                    scores = (
                        lax.dot_general(
                            qm[head, rows, :],
                            keys,
                            (((1,), (1,)), ((), ())),
                            preferred_element_type=jnp.float32,
                        )
                        + bias
                    )
                    old = top[head, rows, :1]
                    new = jnp.maximum(old, jnp.max(scores, axis=1, keepdims=True))
                    weights = jnp.exp(scores - new).astype(jnp.bfloat16)
                    acc[head, rows, :] = acc[head, rows, :] * jnp.exp(old - new) + dot(
                        weights, mixed_vals
                    )
                    top[head, rows, :] = jnp.broadcast_to(new, (big, PAIR))

    for p in range(pairs):
        attend(ctx, p)

    def weight_step(step):
        for line in (wo_line, wp_line):
            for way in range(2):
                line.wait_recv(way, step)

                @pl.when(step + 1 < n_ten - 1)
                def _():
                    line.start(way, step + 1)

    def close(p):
        @pl.loop(0, frames // big)
        def _(i):
            rows = pl.ds(pl.multiple_of(i * big, big), big)
            first, second = acc[2 * p, rows, :], acc[2 * p + 1, rows, :]
            joined = jnp.where(halves[0], first / first[:, HD : HD + 1], second / second[:, :1])
            att[ten, p, rows, :] = joined.astype(jnp.bfloat16)

        for way in range(2):
            at_lines[p].start(way, 0)

    def visit(step, last):
        @pl.when(step < n_ten - 1)
        def _():
            weight_step(step)

        for p in range(pairs):
            for line in ([mk_line] if p == 0 else []) + [kv_lines[p]]:
                for way in range(2):
                    line.wait_recv(way, step)
                    if not last:
                        line.start(way, step + 1)
            for way in range(2):
                slot, live = kv_lines[p].got(way, step)
                pl.when(live)(lambda: attend(slot, p))
            if last:
                close(p)

    @pl.loop(0, n_ctx - 2)
    def _(step):
        visit(step, False)

    visit(n_ctx - 2, True)
    for step in range(n_ctx - 1, n_ten - 1):
        weight_step(step)

    def project(slot, first):
        @pl.loop(0, frames // big)
        def _(i):
            rows = pl.ds(pl.multiple_of(i * big, big), big)
            base = x_ref[rows, :].astype(jnp.float32) if first else total[rows, :]
            total[rows, :] = base + dot(
                jnp.concatenate([att[slot, p, rows, :] for p in range(pairs)], axis=1),
                wo_all[slot],
            )

    project(ten, True)
    for step in range(n_ten - 1):
        for way in range(2):
            for line in at_lines:
                line.wait_recv(way, step)
                if step + 1 < n_ten - 1:
                    line.start(way, step + 1)
        for way in range(2):
            slot, live = at_lines[0].got(way, step)

            @pl.when(live)
            def _():
                project(slot, False)

    @pl.loop(0, frames // chunk)
    def _(i):
        rows = pl.ds(pl.multiple_of(i * chunk, chunk), chunk)
        rounded = total[rows, :].astype(jnp.bfloat16)
        res[rows, :] = rounded
        normed[rows, :] = normalize(rounded, gain2_ref[...])

    loads[5].wait()
    edge = (gpad.shape[0] - frames) // 2

    @pl.loop(0, frames // chunk)
    def _(i):
        rows = pl.ds(pl.multiple_of(i * chunk, chunk), chunk)
        spot = pl.ds(pl.multiple_of(edge + i * chunk, 16), chunk)
        value = dot(normed[rows, :], wp1_ref[0])
        gate = dot(normed[rows, :], wp1_ref[1])
        gated = jnp.where(valid_ref[rows, :] > 0, value * jax.nn.sigmoid(gate), 0.0)
        gpad[spot, :] = gated.astype(jnp.bfloat16)

    def halo(way):
        source = pl.ds(frames, edge) if way == 0 else pl.ds(edge, edge)
        target = pl.ds(0, edge) if way == 0 else pl.ds(frames + edge, edge)
        other = ctx + 1 if way == 0 else ctx + n_ctx - 1
        return pltpu.make_async_remote_copy(
            src_ref=gpad.at[source],
            dst_ref=gpad.at[target],
            send_sem=halo_ss.at[way],
            recv_sem=halo_rs.at[way],
            device_id={"context": lax.rem(other, n_ctx)},
            device_id_type=MESH,
        )

    sends = (ctx < n_ctx - 1, ctx > 0)
    gets = (ctx > 0, ctx < n_ctx - 1)
    for way in range(2):

        @pl.when(sends[way])
        def _():
            halo(way).start()

        @pl.when(jnp.logical_not(gets[way]))
        def _():
            at = 0 if way == 0 else frames + edge
            gpad[at : at + edge, :] = jnp.zeros((edge, cols), jnp.bfloat16)

    g32[edge : edge + frames, :] = gpad[edge : edge + frames, :].astype(jnp.float32)
    for way in range(2):

        @pl.when(gets[way])
        def _():
            halo(way).wait_recv()

        at = 0 if way == 0 else frames + edge
        g32[at : at + edge, :] = gpad[at : at + edge, :].astype(jnp.float32)

    taps = wd_ref.shape[0]
    half = (taps - 1) // 2
    some = min(frames, 64)

    @pl.loop(0, frames // some)
    def _(i):
        start = pl.multiple_of(i * some, some)
        window = g32[pl.ds(start, some + 2 * edge), :]
        depth = jnp.zeros((some, cols), jnp.float32)
        for tap in range(taps):
            at = edge - half + tap
            depth = depth + window[at : at + some, :] * wd_ref[tap : tap + 1, :]
        depth = depth * bns_ref[...] + bnb_ref[...]
        act[pl.ds(start, some), :] = jax.nn.silu(depth).astype(jnp.bfloat16)

    def part(peer):
        return pl.ds(pl.multiple_of(peer * share, share), share)

    def swap(shift):
        peer = lax.rem(ten + shift, n_ten)
        return pltpu.make_async_remote_copy(
            src_ref=act.at[part(peer)],
            dst_ref=act_all.at[shift],
            send_sem=act_ss.at[shift],
            recv_sem=act_rs.at[shift],
            device_id={"tensor": peer},
            device_id_type=MESH,
        )

    for shift in range(1, n_ten):
        swap(shift).start()
    mine = part(ten)
    out = res[mine, :].astype(jnp.float32)
    out = out + dot(act[mine, :], wp2_all[ten])
    for shift in range(1, n_ten):
        swap(shift).wait_recv()
        out = out + dot(act_all[shift], wp2_all[lax.rem(ten + n_ten - shift, n_ten)])
    out_ref[...] = out.astype(jnp.bfloat16)

    for line in kv_lines + at_lines + [mk_line, wo_line, wp_line]:
        line.finish()
    for way in range(2):

        @pl.when(sends[way])
        def _():
            halo(way).wait_send()

    for shift in range(1, n_ten):
        swap(shift).wait_send()


def local(
    n_ctx,
    n_ten,
    inputs,
    frame_valid,
    norm1_gain,
    w_query,
    w_key,
    w_value,
    w_out,
    norm2_gain,
    w_point1,
    w_depth,
    bn_scale,
    bn_shift,
    w_point2,
):
    frames, width = inputs.shape
    cols = w_query.shape[1]
    heads = cols // HD
    share = frames // n_ten
    strips = frames // cols
    edge = 16
    mask = jnp.where(frame_valid > 0, 0.0, NEG).astype(jnp.bfloat16).reshape(strips, cols)
    mask = jnp.pad(mask, ((0, 16 - strips), (0, 0)))
    valid = frame_valid.astype(jnp.float32)[:, None]
    bf, f32 = jnp.bfloat16, jnp.float32
    sem = pltpu.SemaphoreType.DMA
    line = (
        [sem((cols // PAIR, 2, n_ctx - 1))] * 2
        + [sem((2, n_ctx - 1))] * 2
        + [sem((2, n_ten - 1))] * 4
        + [sem((cols // PAIR, 2, n_ten - 1))] * 2
    )
    return pl.pallas_call(
        functools.partial(kernel, n_ctx, n_ten),
        out_shape=jax.ShapeDtypeStruct((share, width), bf),
        in_specs=[pl.BlockSpec(memory_space=pl.ANY if i in (0, 4, 5, 6, 7, 9, 13) else pltpu.VMEM) for i in range(14)],
        out_specs=pl.BlockSpec(memory_space=pltpu.VMEM),
        scratch_shapes=[
            pltpu.VMEM((frames, width), bf),
            pltpu.VMEM((width, cols), bf),
            pltpu.VMEM((width, cols), bf),
            pltpu.VMEM((width, cols), bf),
            pltpu.VMEM((2, width, cols), bf),
            sem((7,)),
            pltpu.VMEM((n_ctx, 16, cols), bf),
            pltpu.VMEM((frames, width), bf),
            pltpu.VMEM((heads, frames, PAIR), bf),
            pltpu.VMEM((n_ctx, cols // PAIR, 2 * frames, PAIR), bf),
            pltpu.VMEM((n_ten, cols, width), bf),
            pltpu.VMEM((n_ten, cols, width), bf),
            pltpu.VMEM((n_ten, cols // PAIR, frames, PAIR), bf),
            pltpu.VMEM((heads, frames, PAIR), f32),
            pltpu.VMEM((heads, frames, PAIR), f32),
            pltpu.VMEM((frames, width), f32),
            pltpu.VMEM((frames, width), bf),
            pltpu.VMEM((frames + 2 * edge, cols), bf),
            pltpu.VMEM((frames + 2 * edge, cols), f32),
            pltpu.VMEM((frames, cols), bf),
            pltpu.VMEM((n_ten, share, cols), bf),
        ]
        + line
        + [sem((2,)), sem((2,)), sem((n_ten,)), sem((n_ten,))],
        compiler_params=pltpu.CompilerParams(
            collective_id=0, has_side_effects=True, vmem_limit_bytes=60 * 1024 * 1024
        ),
    )(
        inputs,
        mask,
        valid,
        norm1_gain[None],
        w_query,
        w_key,
        w_value,
        w_out,
        norm2_gain[None],
        w_point1,
        w_depth,
        bn_scale[None],
        bn_shift[None],
        w_point2,
    )


def solution(mesh):
    placed = (
        P(("groups", "context"), None),
        P(("groups", "context")),
        P(),
        P(None, "tensor"),
        P(None, "tensor"),
        P(None, "tensor"),
        P("tensor", None),
        P(),
        P(None, None, "tensor"),
        P(None, "tensor"),
        P("tensor"),
        P("tensor"),
        P("tensor", None),
    )
    return jax.shard_map(
        functools.partial(local, mesh.shape["context"], mesh.shape["tensor"]),
        mesh=mesh,
        in_specs=placed,
        out_specs=P(("groups", "context", "tensor"), None),
        check_vma=False,
    )
```

```python
import functools
import math

import jax
import jax.numpy as jnp
from jax import lax
from jax.experimental import pallas as pl
from jax.experimental.pallas import tpu as pltpu
from jax.sharding import PartitionSpec as P

HD = 64
NEG = -1e30
PAIR = 128
MESH = pl.DeviceIdType.MESH


def normalize(rows, gain):
    values = rows.astype(jnp.float32)
    center = jnp.mean(values, axis=-1, keepdims=True)
    moved = values - center
    spread = jnp.mean(jnp.square(moved), axis=-1, keepdims=True)
    return (moved * lax.rsqrt(spread + 1e-05) * gain).astype(jnp.bfloat16)


def dot(a, b):
    return jnp.dot(a, b, preferred_element_type=jnp.float32)


class Line:
    def __init__(self, axis, count, pick, send_sems, recv_sems):
        self.axis, self.count, self.pick = axis, count, pick
        self.send_sems, self.recv_sems = send_sems, recv_sems
        self.me = lax.axis_index(axis)

    def sent(self, way, step):
        if way == 0:
            return self.me - step, (self.me >= step) & (self.me < self.count - 1)
        return self.me + step, (self.me + step < self.count) & (self.me > 0)

    def got(self, way, step):
        if way == 0:
            return self.me - 1 - step, self.me >= 1 + step
        return self.me + 1 + step, self.me + 1 + step < self.count

    def copy(self, way, step, slot):
        other = self.me + 1 if way == 0 else self.me + self.count - 1
        return pltpu.make_async_remote_copy(
            src_ref=self.pick(slot),
            dst_ref=self.pick(slot),
            send_sem=self.send_sems.at[way, step],
            recv_sem=self.recv_sems.at[way, step],
            device_id={self.axis: lax.rem(other, self.count)},
            device_id_type=MESH,
        )

    def start(self, way, step):
        slot, live = self.sent(way, step)

        @pl.when(live)
        def _():
            self.copy(way, step, slot).start()

    def wait_send(self, way, step):
        slot, live = self.sent(way, step)

        @pl.when(live)
        def _():
            self.copy(way, step, slot).wait_send()

    def wait_recv(self, way, step):
        slot, live = self.got(way, step)

        @pl.when(live)
        def _():
            self.copy(way, step, slot).wait_recv()

        return slot, live

    def finish(self):
        for way in range(2):

            @pl.loop(0, self.count - 1)
            def _(step):
                self.wait_send(way, step)


def kernel(
    n_ctx,
    n_ten,
    x_hbm,
    mask_ref,
    valid_ref,
    gain1_ref,
    wq_hbm,
    wk_hbm,
    wv_hbm,
    wo_hbm,
    gain2_ref,
    wp1_hbm,
    wd_ref,
    bns_ref,
    bnb_ref,
    wp2_hbm,
    out_ref,
    x_ref,
    wq_ref,
    wk_ref,
    wv_ref,
    wp1_ref,
    load,
    masks,
    normed,
    qm,
    kv,
    wo_all,
    wp2_all,
    att,
    acc,
    top,
    total,
    res,
    gpad,
    g32,
    act,
    act_all,
    kv_ss,
    kv_rs,
    mk_ss,
    mk_rs,
    wo_ss,
    wo_rs,
    wp_ss,
    wp_rs,
    at_ss,
    at_rs,
    halo_ss,
    halo_rs,
    act_ss,
    act_rs,
):
    ctx = lax.axis_index("context")
    ten = lax.axis_index("tensor")
    frames, width = x_ref.shape
    cols = wq_ref.shape[1]
    pairs = cols // PAIR
    share = frames // n_ten
    chunk = min(frames, 128)

    barrier = pltpu.get_barrier_semaphore()
    for shift in (1, n_ctx - 1):
        pl.semaphore_signal(
            barrier, inc=1, device_id={"context": lax.rem(ctx + shift, n_ctx)}, device_id_type=MESH
        )
    for shift in range(1, n_ten):
        pl.semaphore_signal(
            barrier, inc=1, device_id={"tensor": lax.rem(ten + shift, n_ten)}, device_id_type=MESH
        )
    loads = [
        pltpu.make_async_copy(source, target, load.at[i])
        for i, (source, target) in enumerate(
            (
                (x_hbm, x_ref),
                (wk_hbm, wk_ref),
                (wv_hbm, wv_ref),
                (wq_hbm, wq_ref),
                (wo_hbm, wo_all.at[ten]),
                (wp1_hbm, wp1_ref),
                (wp2_hbm, wp2_all.at[ten]),
            )
        )
    ]
    for item in loads:
        item.start()

    def pair_line(axis, count, slots, p, send_sems, recv_sems):
        return Line(axis, count, lambda slot: slots.at[slot, p], send_sems.at[p], recv_sems.at[p])

    kv_lines = [pair_line("context", n_ctx, kv, p, kv_ss, kv_rs) for p in range(pairs)]
    at_lines = [pair_line("tensor", n_ten, att, p, at_ss, at_rs) for p in range(pairs)]
    mk_line = Line("context", n_ctx, lambda slot: masks.at[slot], mk_ss, mk_rs)
    wo_line = Line("tensor", n_ten, lambda slot: wo_all.at[slot], wo_ss, wo_rs)
    wp_line = Line("tensor", n_ten, lambda slot: wp2_all.at[slot], wp_ss, wp_rs)
    masks[ctx] = mask_ref[...]
    loads[0].wait()

    big = min(frames, 256)
    loads[1].wait()
    loads[2].wait()

    @pl.loop(0, frames // chunk, unroll=True)
    def _(i):
        rows = pl.ds(pl.multiple_of(i * chunk, chunk), chunk)
        low = pl.ds(pl.multiple_of(frames + i * chunk, chunk), chunk)
        part = normalize(x_ref[rows, :], gain1_ref[...])
        normed[rows, :] = part
        keys = dot(part, wk_ref[...]).astype(jnp.bfloat16)
        vals = dot(part, wv_ref[...]).astype(jnp.bfloat16)
        for p in range(pairs):
            kv[ctx, p, rows, :] = keys[:, p * PAIR : (p + 1) * PAIR]
            kv[ctx, p, low, :] = vals[:, p * PAIR : (p + 1) * PAIR]

    pl.semaphore_wait(barrier, 2 + n_ten - 1)
    for line in [mk_line] + kv_lines:
        for way in range(2):
            line.start(way, 0)
    loads[4].wait()
    loads[6].wait()
    for line in (wo_line, wp_line):
        for way in range(2):
            line.start(way, 0)
    loads[3].wait()

    lane = lax.broadcasted_iota(jnp.int32, (1, PAIR), 1)
    halves = (lane < HD, lane >= HD)

    @pl.loop(0, frames // big, unroll=True)
    def _(i):
        rows = pl.ds(pl.multiple_of(i * big, big), big)
        query = (dot(normed[rows, :], wq_ref[...]).astype(jnp.bfloat16)) * jnp.bfloat16(
            1.0 / math.sqrt(HD)
        )
        for p in range(pairs):
            part = query[:, p * PAIR : (p + 1) * PAIR]
            for h in range(2):
                qm[2 * p + h, rows, :] = jnp.where(halves[h], part, jnp.bfloat16(0))

    top[...] = jnp.full_like(top, NEG)
    acc[...] = jnp.zeros_like(acc)

    def attend(block, p):
        strip = masks[block].astype(jnp.float32)
        bias = jnp.concatenate([strip[i : i + 1, :] for i in range(frames // cols)], axis=1)
        if True:
            keys = kv[block, p, :frames, :]
            vals = kv[block, p, frames:, :]
            for h in range(2):
                head = 2 * p + h
                mixed_vals = jnp.where(halves[h], vals, jnp.bfloat16(1))

                @pl.loop(0, frames // big, unroll=True)
                def _(i):
                    rows = pl.ds(pl.multiple_of(i * big, big), big)
                    scores = (
                        lax.dot_general(
                            qm[head, rows, :],
                            keys,
                            (((1,), (1,)), ((), ())),
                            preferred_element_type=jnp.float32,
                        )
                        + bias
                    )
                    old = top[head, rows, :1]
                    new = jnp.maximum(old, jnp.max(scores, axis=1, keepdims=True))
                    weights = jnp.exp(scores - new).astype(jnp.bfloat16)
                    acc[head, rows, :] = acc[head, rows, :] * jnp.exp(old - new) + dot(
                        weights, mixed_vals
                    )
                    top[head, rows, :] = jnp.broadcast_to(new, (big, PAIR))

    for p in range(pairs):
        attend(ctx, p)

    def weight_step(step):
        for line in (wo_line, wp_line):
            for way in range(2):
                line.wait_recv(way, step)

                @pl.when(step + 1 < n_ten - 1)
                def _():
                    line.start(way, step + 1)

    def close(p):
        @pl.loop(0, frames // big, unroll=True)
        def _(i):
            rows = pl.ds(pl.multiple_of(i * big, big), big)
            first, second = acc[2 * p, rows, :], acc[2 * p + 1, rows, :]
            joined = jnp.where(halves[0], first / first[:, HD : HD + 1], second / second[:, :1])
            att[ten, p, rows, :] = joined.astype(jnp.bfloat16)

        for way in range(2):
            at_lines[p].start(way, 0)

    def visit(step, last):
        @pl.when(step < n_ten - 1)
        def _():
            weight_step(step)

        for p in range(pairs):
            for line in ([mk_line] if p == 0 else []) + [kv_lines[p]]:
                for way in range(2):
                    line.wait_recv(way, step)
                    if not last:
                        line.start(way, step + 1)
            for way in range(2):
                slot, live = kv_lines[p].got(way, step)
                pl.when(live)(lambda: attend(slot, p))
            if last:
                close(p)

    @pl.loop(0, n_ctx - 2)
    def _(step):
        visit(step, False)

    visit(n_ctx - 2, True)
    for step in range(n_ctx - 1, n_ten - 1):
        weight_step(step)

    def project(slot, first):
        @pl.loop(0, frames // big, unroll=True)
        def _(i):
            rows = pl.ds(pl.multiple_of(i * big, big), big)
            base = x_ref[rows, :].astype(jnp.float32) if first else total[rows, :]
            total[rows, :] = base + dot(
                jnp.concatenate([att[slot, p, rows, :] for p in range(pairs)], axis=1),
                wo_all[slot],
            )

    project(ten, True)
    for step in range(n_ten - 1):
        for way in range(2):
            for line in at_lines:
                line.wait_recv(way, step)
                if step + 1 < n_ten - 1:
                    line.start(way, step + 1)
        for way in range(2):
            slot, live = at_lines[0].got(way, step)

            @pl.when(live)
            def _():
                project(slot, False)

    loads[5].wait()
    edge = (gpad.shape[0] - frames) // 2

    @pl.loop(0, frames // chunk, unroll=True)
    def _(i):
        rows = pl.ds(pl.multiple_of(i * chunk, chunk), chunk)
        spot = pl.ds(pl.multiple_of(edge + i * chunk, 16), chunk)
        rounded = total[rows, :].astype(jnp.bfloat16)
        res[rows, :] = rounded
        part = normalize(rounded, gain2_ref[...])
        value = dot(part, wp1_ref[0])
        gate = dot(part, wp1_ref[1])
        gated = jnp.where(valid_ref[rows, :] > 0, value * jax.nn.sigmoid(gate), 0.0)
        gpad[spot, :] = gated.astype(jnp.bfloat16)

    def halo(way):
        source = pl.ds(frames, edge) if way == 0 else pl.ds(edge, edge)
        target = pl.ds(0, edge) if way == 0 else pl.ds(frames + edge, edge)
        other = ctx + 1 if way == 0 else ctx + n_ctx - 1
        return pltpu.make_async_remote_copy(
            src_ref=gpad.at[source],
            dst_ref=gpad.at[target],
            send_sem=halo_ss.at[way],
            recv_sem=halo_rs.at[way],
            device_id={"context": lax.rem(other, n_ctx)},
            device_id_type=MESH,
        )

    sends = (ctx < n_ctx - 1, ctx > 0)
    gets = (ctx > 0, ctx < n_ctx - 1)
    for way in range(2):

        @pl.when(sends[way])
        def _():
            halo(way).start()

        @pl.when(jnp.logical_not(gets[way]))
        def _():
            at = 0 if way == 0 else frames + edge
            gpad[at : at + edge, :] = jnp.zeros((edge, cols), jnp.bfloat16)

    g32[edge : edge + frames, :] = gpad[edge : edge + frames, :].astype(jnp.float32)
    for way in range(2):

        @pl.when(gets[way])
        def _():
            halo(way).wait_recv()

        at = 0 if way == 0 else frames + edge
        g32[at : at + edge, :] = gpad[at : at + edge, :].astype(jnp.float32)

    taps = wd_ref.shape[0]
    half = (taps - 1) // 2
    some = min(frames, 64)

    @pl.loop(0, frames // some)
    def _(i):
        start = pl.multiple_of(i * some, some)
        window = g32[pl.ds(start, some + 2 * edge), :]
        depth = jnp.zeros((some, cols), jnp.float32)
        for tap in range(taps):
            at = edge - half + tap
            depth = depth + window[at : at + some, :] * wd_ref[tap : tap + 1, :]
        depth = depth * bns_ref[...] + bnb_ref[...]
        act[pl.ds(start, some), :] = jax.nn.silu(depth).astype(jnp.bfloat16)

    def part(peer):
        return pl.ds(pl.multiple_of(peer * share, share), share)

    def swap(shift):
        peer = lax.rem(ten + shift, n_ten)
        return pltpu.make_async_remote_copy(
            src_ref=act.at[part(peer)],
            dst_ref=act_all.at[shift],
            send_sem=act_ss.at[shift],
            recv_sem=act_rs.at[shift],
            device_id={"tensor": peer},
            device_id_type=MESH,
        )

    for shift in range(1, n_ten):
        swap(shift).start()
    mine = part(ten)
    out = res[mine, :].astype(jnp.float32)
    out = out + dot(act[mine, :], wp2_all[ten])
    for shift in range(1, n_ten):
        swap(shift).wait_recv()
        out = out + dot(act_all[shift], wp2_all[lax.rem(ten + n_ten - shift, n_ten)])
    out_ref[...] = out.astype(jnp.bfloat16)

    for line in kv_lines + at_lines + [mk_line, wo_line, wp_line]:
        line.finish()
    for way in range(2):

        @pl.when(sends[way])
        def _():
            halo(way).wait_send()

    for shift in range(1, n_ten):
        swap(shift).wait_send()


def local(
    n_ctx,
    n_ten,
    inputs,
    frame_valid,
    norm1_gain,
    w_query,
    w_key,
    w_value,
    w_out,
    norm2_gain,
    w_point1,
    w_depth,
    bn_scale,
    bn_shift,
    w_point2,
):
    frames, width = inputs.shape
    cols = w_query.shape[1]
    heads = cols // HD
    share = frames // n_ten
    strips = frames // cols
    edge = 16
    mask = jnp.where(frame_valid > 0, 0.0, NEG).astype(jnp.bfloat16).reshape(strips, cols)
    mask = jnp.pad(mask, ((0, 16 - strips), (0, 0)))
    valid = frame_valid.astype(jnp.float32)[:, None]
    bf, f32 = jnp.bfloat16, jnp.float32
    sem = pltpu.SemaphoreType.DMA
    line = (
        [sem((cols // PAIR, 2, n_ctx - 1))] * 2
        + [sem((2, n_ctx - 1))] * 2
        + [sem((2, n_ten - 1))] * 4
        + [sem((cols // PAIR, 2, n_ten - 1))] * 2
    )
    return pl.pallas_call(
        functools.partial(kernel, n_ctx, n_ten),
        out_shape=jax.ShapeDtypeStruct((share, width), bf),
        in_specs=[pl.BlockSpec(memory_space=pl.ANY if i in (0, 4, 5, 6, 7, 9, 13) else pltpu.VMEM) for i in range(14)],
        out_specs=pl.BlockSpec(memory_space=pltpu.VMEM),
        scratch_shapes=[
            pltpu.VMEM((frames, width), bf),
            pltpu.VMEM((width, cols), bf),
            pltpu.VMEM((width, cols), bf),
            pltpu.VMEM((width, cols), bf),
            pltpu.VMEM((2, width, cols), bf),
            sem((7,)),
            pltpu.VMEM((n_ctx, 16, cols), bf),
            pltpu.VMEM((frames, width), bf),
            pltpu.VMEM((heads, frames, PAIR), bf),
            pltpu.VMEM((n_ctx, cols // PAIR, 2 * frames, PAIR), bf),
            pltpu.VMEM((n_ten, cols, width), bf),
            pltpu.VMEM((n_ten, cols, width), bf),
            pltpu.VMEM((n_ten, cols // PAIR, frames, PAIR), bf),
            pltpu.VMEM((heads, frames, PAIR), f32),
            pltpu.VMEM((heads, frames, PAIR), f32),
            pltpu.VMEM((frames, width), f32),
            pltpu.VMEM((frames, width), bf),
            pltpu.VMEM((frames + 2 * edge, cols), bf),
            pltpu.VMEM((frames + 2 * edge, cols), f32),
            pltpu.VMEM((frames, cols), bf),
            pltpu.VMEM((n_ten, share, cols), bf),
        ]
        + line
        + [sem((2,)), sem((2,)), sem((n_ten,)), sem((n_ten,))],
        compiler_params=pltpu.CompilerParams(
            collective_id=0, has_side_effects=True, vmem_limit_bytes=60 * 1024 * 1024
        ),
    )(
        inputs,
        mask,
        valid,
        norm1_gain[None],
        w_query,
        w_key,
        w_value,
        w_out,
        norm2_gain[None],
        w_point1,
        w_depth,
        bn_scale[None],
        bn_shift[None],
        w_point2,
    )


def solution(mesh):
    placed = (
        P(("groups", "context"), None),
        P(("groups", "context")),
        P(),
        P(None, "tensor"),
        P(None, "tensor"),
        P(None, "tensor"),
        P("tensor", None),
        P(),
        P(None, None, "tensor"),
        P(None, "tensor"),
        P("tensor"),
        P("tensor"),
        P("tensor", None),
    )
    return jax.shard_map(
        functools.partial(local, mesh.shape["context"], mesh.shape["tensor"]),
        mesh=mesh,
        in_specs=placed,
        out_specs=P(("groups", "context", "tensor"), None),
        check_vma=False,
    )
```
